256 devices in a mesh: wide: 32 (over y, z), narrow: 8 (over x, core).
Axes of the slice: x: 4, y: 4, z: 8, core: 2. Of those that a mesh axis runs over, the one named last changes fastest.
Arguments:
- targets: float32 [262144, 64], P(('wide', 'narrow')), may hold values from -6 to 6
- train_features: bfloat16 [262144, 128], P(('wide', 'narrow')), may hold values from -6 to 6
- test_features: bfloat16 [8192, 128], P(('wide', 'narrow')), may hold values from -6 to 6
- left_factors: float32 [262144, 4, 128], P(('wide', 'narrow')), may hold values from -0.5 to 0.5
- right_factors: float32 [262144, 4, 128], P(('wide', 'narrow')), may hold values from -0.01171875 to 0.01171875
- capacitance: float32 [15, 256, 256], replicated, may hold values from -0.375 to 0.375
- pivots: int32 [15, 256], replicated, may hold values from 0 to 255, each once within a row
Outputs:
- solved_targets: float32 [262144, 64], P(('wide', 'narrow'))
- predictions: float32 [8192, 64], P(('wide', 'narrow'))
The draws below stay inside these ranges and needn't reach their ends.
Inputs may be any that keep to these rules, and one draw needn't show every extreme that they name: `pivots`: each row is a permutation of 0 .. 255.
All inputs are finite; a program needn't handle non-finite values.
Results may differ from the reference program's by a relative error of at most 0.0049.
Values may be sent and summed in bfloat16 or wider, within the bound.
No kernel may reach another device: no remote copies, remote signals or barrier semaphores. Data moves between devices by JAX's collectives and lax.ppermute only.
A program may use at most 128 MiB of HBM per device.

```python
import jax
import jax.numpy as jnp
from jax import lax

R = 128
FEAT = 128
TARGETS = 64
LEVELS = 4
NODES = 15
POINTS = 262144
TESTS = 8192


def steps_of(own_key, extent, pieces, low, top_value):
    factor_of = 1.0
    for dim, shards_of in pieces:
        steps = jax.random.uniform(jax.random.fold_in(jax.random.fold_in(own_key, 6), dim), (shards_of,), jnp.float32, low / len(pieces), top_value / len(pieces))
        factor_of = factor_of * jnp.repeat(jnp.exp(steps), extent[dim] // shards_of).reshape((-1,) + (1,) * (len(extent) - 1 - dim))
    return factor_of


def bell_draw(own_key, extent, scale, most, shards=(), kind=jnp.bfloat16):
    entries = jax.random.normal(own_key, extent, jnp.float32) * scale
    if len(shards) > 0:
        entries = steps_of(own_key, extent, shards, -0.22, 0.18) * entries
    return jnp.clip(entries, min=-most, max=most).astype(kind)


def setup_inputs(seed: int = 0) -> dict:
    key_of = jax.random.split(jax.random.key(seed), 8)
    return {
        "targets": bell_draw(key_of[0], (POINTS, TARGETS), 1.0, 6.0, ((0, 256),), jnp.float32),
        "train_features": bell_draw(key_of[1], (POINTS, FEAT), 1.0, 6.0, ((0, 256),)),
        "test_features": bell_draw(key_of[2], (TESTS, FEAT), 1.0, 6.0, ((0, 256),)),
        "left_factors": bell_draw(key_of[3], (POINTS, LEVELS, R), R ** -0.5, 0.5, ((0, 256),), jnp.float32),
        "right_factors": bell_draw(key_of[4], (POINTS, LEVELS, R), POINTS ** -0.5, 0.01171875, ((0, 256),), jnp.float32),
        "capacitance": bell_draw(key_of[5], (NODES, 2 * R, 2 * R), (2 * R) ** -0.5, 0.375, (), jnp.float32),
        "pivots": jax.vmap(lambda own: jax.random.permutation(own, 2 * R))(jax.random.split(key_of[6], NODES)).reshape((NODES, 2 * R)).astype(jnp.int32),
    }


spread_coef = 3.0


def level_update(current, left_level, right_level, capacitance, pivots, tree_level):
    children = 2 ** tree_level
    nodes = children // 2
    offset = nodes - 1
    per_child = POINTS // children
    right_blocks = right_level.reshape(children, per_child, R)
    left_blocks = left_level.reshape(children, per_child, R)
    value_blocks = current.reshape(children, per_child, TARGETS)
    projected = jnp.einsum("cpr,cpt->crt", right_blocks, value_blocks, precision=lax.Precision.HIGHEST)
    paired = projected.reshape(nodes, 2, R, TARGETS)
    stacked = jnp.concatenate([paired[:, 1], paired[:, 0]], axis=1)
    node_pivots = pivots[offset:offset + nodes].astype(jnp.int32)
    permuted = jnp.take_along_axis(stacked, node_pivots[:, :, None], axis=1)
    caps = capacitance[offset:offset + nodes]
    solved = jnp.einsum("nij,njt->nit", caps, permuted, precision=lax.Precision.HIGHEST)
    shares = solved.reshape(children, R, TARGETS)
    update = jnp.einsum("cpr,crt->cpt", left_blocks, shares, precision=lax.Precision.HIGHEST)
    return current - update.reshape(POINTS, TARGETS)


def reference(targets, train_features, test_features, left_factors, right_factors, capacitance, pivots):
    current = targets.astype(jnp.float32)
    for tree_level in range(1, LEVELS + 1):
        current = level_update(current, left_factors[:, tree_level - 1, :], right_factors[:, tree_level - 1, :], capacitance, pivots, tree_level)
    weights_bf = current.astype(jnp.bfloat16)
    train_float = train_features.astype(jnp.float32)
    train_sq = jnp.sum(train_float * train_float, axis=1)
    block_rows = 128 if TESTS % 128 == 0 else TESTS
    blocks = test_features.reshape(TESTS // block_rows, block_rows, FEAT)

    def predict_block(rows_in):
        rows_float = rows_in.astype(jnp.float32)
        row_sq = jnp.sum(rows_float * rows_float, axis=1)
        inner = lax.dot_general(rows_in, train_features, (((1,), (1,)), ((), ())), preferred_element_type=jnp.float32)
        dist = row_sq[:, None] + train_sq[None, :] - 2.0 * inner
        kernel = jnp.exp(-(spread_coef / FEAT) * dist).astype(jnp.bfloat16)
        return jnp.dot(kernel, weights_bf, preferred_element_type=jnp.float32)

    predictions = lax.map(predict_block, blocks).reshape(TESTS, TARGETS)
    return current, predictions
```

```python
import math

import jax
import jax.numpy as jnp
from jax import lax
from jax.experimental import pallas as pl
from jax.experimental.pallas import tpu as pltpu
from jax.sharding import Mesh, PartitionSpec as P

LEVELS = 4
RANK = 128
FEAT = 128
TARGETS = 64
POINTS = 1024
SPREAD = 3.0
CUTS = (0, 8, 32, 72, 128)

f32 = jnp.float32
bf16 = jnp.bfloat16
NT = (((1,), (1,)), ((), ()))
NN = (((1,), (0,)), ((), ()))


def params(limit=48):
    return pltpu.CompilerParams(vmem_limit_bytes=limit * 1024 * 1024)


def split2(value):
    high = value.astype(bf16)
    return high, (value - high.astype(f32)).astype(bf16)


def dot3(a, b, dims):
    def one(p, q):
        return lax.dot_general(p, q, dims, preferred_element_type=f32)

    return one(a[0], b[0]) + (one(a[0], b[1]) + one(a[1], b[0]))


def gram_kernel(targets_ref, left_ref, right_ref, tests_ref, out_ref, upper, lower):
    step = pl.program_id(0)
    count = targets_ref.shape[1]

    def level(ref, index):
        return ref[pl.ds(index, count, stride=LEVELS), :]

    rows = jnp.concatenate([targets_ref[...]] + [level(left_ref, k).T for k in range(3)], axis=0)
    high, low = split2(rows)
    right = [split2(level(right_ref, k)) for k in range(4)]
    pair = lambda i, j: tuple(jnp.concatenate([right[i][p], right[j][p]], axis=1) for p in (0, 1))
    first = dot3((high[:192], low[:192]), pair(0, 1), NN)
    second = dot3((high, low), pair(2, 3), NN)

    @pl.when(step == 0)
    def _():
        upper[...] = first
        lower[...] = second

    @pl.when(step > 0)
    def _():
        upper[...] += first
        lower[...] += second

    @pl.when(step == pl.num_programs(0) - 1)
    def _():
        for n in range(8):
            block = jnp.concatenate(
                [
                    upper[8 * n : 8 * n + 8, :RANK],
                    upper[24 * n : 24 * n + 24, RANK:],
                    lower[40 * n : 40 * n + 40, :RANK],
                    lower[56 * n : 56 * n + 56, RANK:],
                ],
                axis=0,
            )
            out_ref[n, :128] = block.astype(bf16)
            out_ref[n, 128:] = tests_ref[...]


def gram(targets_t, left, right, tests):
    chunk = 256
    return pl.pallas_call(
        gram_kernel,
        grid=(POINTS // chunk,),
        in_specs=[
            pl.BlockSpec((TARGETS, chunk), lambda i: (0, i)),
            pl.BlockSpec((LEVELS * chunk, RANK), lambda i: (i, 0)),
            pl.BlockSpec((LEVELS * chunk, RANK), lambda i: (i, 0)),
            pl.BlockSpec((32, FEAT), lambda i: (0, 0)),
        ],
        out_specs=pl.BlockSpec((8, 160, RANK), lambda i: (0, 0, 0)),
        out_shape=jax.ShapeDtypeStruct((8, 160, RANK), bf16),
        scratch_shapes=[pltpu.VMEM((192, 256), f32), pltpu.VMEM((448, 256), f32)],
        compiler_params=params(),
        name="gram",
    )(targets_t, left, right, tests)


def block_sum_kernel(where, in_ref, out_ref):
    core = where[8]
    total = in_ref[0, :128].astype(f32)
    for n in range(1, 8):
        total += in_ref[n, :128].astype(f32)
    total = total.astype(bf16)
    tests = [in_ref[2 * x + core, 128:] for x in range(4)]
    for n in range(8):
        out_ref[n, :128] = total
        for x in range(4):
            out_ref[n, 128 + 32 * x : 160 + 32 * x] = tests[x]


def block_sum(where, arrived):
    return pl.pallas_call(
        block_sum_kernel,
        grid_spec=pltpu.PrefetchScalarGridSpec(
            num_scalar_prefetch=1,
            grid=(1,),
            in_specs=[pl.BlockSpec((8, 160, RANK), lambda i, w: (0, 0, 0))],
            out_specs=pl.BlockSpec((8, 256, RANK), lambda i, w: (0, 0, 0)),
        ),
        out_shape=jax.ShapeDtypeStruct((8, 256, RANK), bf16),
        compiler_params=params(),
        name="block_sum",
    )(where, arrived)


def plane_sum_kernel(where, in_ref, send_ref, near_ref, tests_ref):
    z = where[9]
    pair = jnp.right_shift(z, 1)

    def rows(index):
        return in_ref[index, :128].astype(f32)

    whole = [rows(k) for k in range(8)]
    below = (whole[0] + whole[1]) + (whole[2] + whole[3])
    above = (whole[4] + whole[5]) + (whole[6] + whole[7])
    send = (below + above)[:32].astype(bf16)
    for k in range(4):
        send_ref[k] = send
    odd, even = 2 * jnp.bitwise_or(pair, 1), 2 * jnp.bitwise_and(pair, 2)
    near_ref[0, :40] = above[32:72]
    near_ref[1, :40] = below[32:72]
    near_ref[0, 40:] = (rows(odd) + rows(odd + 1))[72:]
    near_ref[1, 40:] = (rows(even) + rows(even + 1))[72:]
    for k in range(8):
        tests_ref[128 * k : 128 * k + 128] = in_ref[k, 128:]


def plane_sum(where, arrived):
    return pl.pallas_call(
        plane_sum_kernel,
        grid_spec=pltpu.PrefetchScalarGridSpec(
            num_scalar_prefetch=1,
            grid=(1,),
            in_specs=[pl.BlockSpec((8, 256, RANK), lambda i, w: (0, 0, 0))],
            out_specs=[
                pl.BlockSpec((4, 32, RANK), lambda i, w: (0, 0, 0)),
                pl.BlockSpec((2, 96, RANK), lambda i, w: (0, 0, 0)),
                pl.BlockSpec((1024, FEAT), lambda i, w: (0, 0)),
            ],
        ),
        out_shape=[
            jax.ShapeDtypeStruct((4, 32, RANK), bf16),
            jax.ShapeDtypeStruct((2, 96, RANK), f32),
            jax.ShapeDtypeStruct((1024, FEAT), bf16),
        ],
        compiler_params=params(),
        name="plane_sum",
    )(where, arrived)


def node_kernel(where, far_ref, near_ref, *refs):
    caps, pivots, out_ref = refs[:4], refs[4:8], refs[8]
    y = where[10]

    def far(index):
        return far_ref[index].astype(f32)

    stacks = [
        ((far(2) + far(3))[:8], (far(0) + far(1))[:8]),
        (far(jnp.bitwise_or(y, 1))[8:], far(jnp.bitwise_and(y, 2))[8:]),
        (near_ref[0, :40], near_ref[1, :40]),
        (near_ref[0, 40:], near_ref[1, 40:]),
    ]
    solved = []
    for level in range(LEVELS):
        stacked = split2(jnp.concatenate(stacks[level], axis=1))
        source = lax.broadcasted_iota(jnp.int32, (256, 256), 0)
        picks = jnp.where(source == pivots[level][0], 1.0, 0.0).astype(bf16)
        moved = [
            lax.dot_general(piece, picks, NN, preferred_element_type=f32).astype(bf16)
            for piece in stacked
        ]
        solved.append(dot3(moved, split2(caps[level][0]), NT))
    block = jnp.concatenate(solved, axis=0).astype(bf16)
    for n in range(8):
        out_ref[n] = block


def node_solve(where, far, near, capacitance, pivots):
    cap_specs = [
        pl.BlockSpec((1, RANK, 2 * RANK), lambda i, w, k=k: (w[k], w[4 + k], 0)) for k in range(4)
    ]
    pivot_specs = [
        pl.BlockSpec((1, 1, 2 * RANK), lambda i, w, k=k: (w[k], 0, 0)) for k in range(4)
    ]
    return pl.pallas_call(
        node_kernel,
        grid_spec=pltpu.PrefetchScalarGridSpec(
            num_scalar_prefetch=1,
            grid=(1,),
            in_specs=[
                pl.BlockSpec((4, 32, RANK), lambda i, w: (0, 0, 0)),
                pl.BlockSpec((2, 96, RANK), lambda i, w: (0, 0, 0)),
            ]
            + cap_specs
            + pivot_specs,
            out_specs=pl.BlockSpec((8, 128, RANK), lambda i, w: (0, 0, 0)),
        ),
        out_shape=jax.ShapeDtypeStruct((8, 128, RANK), bf16),
        compiler_params=params(),
        name="node_solve",
    )(where, far, near, *([capacitance] * 4), *([pivots] * 4))


def update_kernel(pieces_ref, targets_ref, left_ref, out_ref, weights_ref, shares_high, shares_low):
    count = targets_ref.shape[1]

    @pl.when(pl.program_id(0) == 0)
    def _():
        pieces = [pieces_ref[n].astype(f32) for n in range(8)]
        shares = []
        for level in range(LEVELS):
            rows = jnp.concatenate([p[CUTS[level] : CUTS[level + 1]] for p in pieces], axis=0)
            share = rows[:TARGETS]
            for k in range(level):
                begin = TARGETS + RANK * k
                share -= dot3(shares[k], split2(rows[begin : begin + RANK]), NN)
            shares.append(split2(share))
        shares_high[...] = jnp.concatenate([s[0] for s in shares], axis=1)
        shares_low[...] = jnp.concatenate([s[1] for s in shares], axis=1)

    left = [split2(left_ref[pl.ds(k, count, stride=LEVELS), :]) for k in range(LEVELS)]
    joined = [jnp.concatenate([part[p] for part in left], axis=1) for p in (0, 1)]
    value = targets_ref[...] - dot3((shares_high[...], shares_low[...]), joined, NT)
    out_ref[...] = value
    weights_ref[...] = value.astype(bf16)


def update(pieces, targets_t, left):
    chunk = 256
    return pl.pallas_call(
        update_kernel,
        grid=(POINTS // chunk,),
        in_specs=[
            pl.BlockSpec((8, 128, RANK), lambda i: (0, 0, 0)),
            pl.BlockSpec((TARGETS, chunk), lambda i: (0, i)),
            pl.BlockSpec((LEVELS * chunk, RANK), lambda i: (i, 0)),
        ],
        out_specs=[
            pl.BlockSpec((TARGETS, chunk), lambda i: (0, i)),
            pl.BlockSpec((TARGETS, chunk), lambda i: (0, i)),
        ],
        out_shape=[
            jax.ShapeDtypeStruct((TARGETS, POINTS), f32),
            jax.ShapeDtypeStruct((TARGETS, POINTS), bf16),
        ],
        scratch_shapes=[
            pltpu.VMEM((TARGETS, LEVELS * RANK), bf16),
            pltpu.VMEM((TARGETS, LEVELS * RANK), bf16),
        ],
        compiler_params=params(),
        name="update",
    )(pieces, targets_t, left)


def widened(points, norm_at, one_at):
    value = points.astype(f32)
    norm = -0.5 * jnp.sum(value * value, axis=1, keepdims=True)
    high = norm.astype(bf16).astype(f32)
    middle = (norm - high).astype(bf16).astype(f32)
    low = norm - high - middle
    lane = lax.broadcasted_iota(jnp.int32, points.shape, 1)
    extra = jnp.where((lane >= one_at) & (lane < one_at + 3), 1.0, 0.0)
    for k, piece in enumerate((high, middle, low)):
        extra = jnp.where(lane == norm_at + k, piece, extra)
    return jnp.concatenate([points, extra.astype(bf16)], axis=1)


def predict_kernel(where, *refs):
    tests, own_ref, other_ref = refs[:4], refs[4], refs[5]
    own_w, other_w, out_ref, train, weights, block = refs[6:]
    turn, part = pl.program_id(0), pl.program_id(1)

    @pl.when((turn == 0) & (part == 0))
    def _():
        for k, (ref, w) in enumerate(((own_ref, own_w), (other_ref, other_w))):
            for j in range(4):
                at = 1024 * k + 256 * j
                train[at : at + 256] = widened(ref[256 * j : 256 * j + 256], 0, 3)
                weights[at : at + 256] = w[:, 256 * j : 256 * j + 256].astype(f32).T.astype(bf16)

    for k in range(4):

        @pl.when(turn == k)
        def _():
            block[...] = widened(tests[k][...], 3, 0)

    scale = 2.0 * SPREAD / FEAT * math.log2(math.e)
    total = jnp.zeros((256, TARGETS), f32)
    for j in range(8):
        at = 256 * j
        inner = lax.dot_general(block[...], train[at : at + 256], NT, preferred_element_type=f32)
        kernel = jnp.exp2(inner * scale).astype(bf16)
        total += lax.dot_general(kernel, weights[at : at + 256], NN, preferred_element_type=f32)
    for k in range(8):
        rows = [total[32 * k + 16 * h : 32 * k + 16 * h + 16] for h in (0, 1)]
        out_ref[k] = jnp.concatenate(rows, axis=1).astype(bf16)


def predict(where, tests, features, other_features, weights, other_weights):
    def test_spec(k):
        def at(i, j, w):
            return (jnp.where(i == k, j, jnp.where(i < k, 0, 3)), 0)

        return pl.BlockSpec((256, FEAT), at)

    whole = lambda shape: pl.BlockSpec(shape, lambda i, j, w: (0,) * len(shape))
    return pl.pallas_call(
        predict_kernel,
        grid_spec=pltpu.PrefetchScalarGridSpec(
            num_scalar_prefetch=1,
            grid=(4, 4),
            in_specs=[test_spec(k) for k in range(4)]
            + [whole((POINTS, FEAT))] * 2
            + [whole((TARGETS, POINTS))] * 2,
            out_specs=pl.BlockSpec(
                (8, 16, 128), lambda i, j, w: (4 * jnp.bitwise_xor(w[10], i) + j, 0, 0)
            ),
            scratch_shapes=[
                pltpu.VMEM((2 * POINTS, 2 * FEAT), bf16),
                pltpu.VMEM((2 * POINTS, TARGETS), bf16),
                pltpu.VMEM((256, 2 * FEAT), bf16),
            ],
        ),
        out_shape=jax.ShapeDtypeStruct((128, 16, 128), bf16),
        compiler_params=params(),
        name="predict",
    )(where, *tests, features, other_features, weights, other_weights)


def final_kernel(in_ref, out_ref):
    total = in_ref[0].astype(f32)
    for k in range(1, 128):
        total += in_ref[k].astype(f32)
    out_ref[:16] = total[:, :TARGETS]
    out_ref[16:] = total[:, TARGETS:]


def final_sum(arrived):
    return pl.pallas_call(
        final_kernel,
        out_shape=jax.ShapeDtypeStruct((32, TARGETS), f32),
        compiler_params=params(),
        name="final_sum",
    )(arrived)


def exchange(blocks, axes):
    return lax.all_to_all(blocks, axes, 0, 0, tiled=True)


def flipped(value, axis, mask):
    return lax.ppermute(value, axis, [(s, s ^ mask) for s in range(lax.axis_size(axis))])


def body(targets, train_features, test_features, left_factors, right_factors, capacitance, pivots):
    y, z, core = lax.axis_index("y"), lax.axis_index("z"), lax.axis_index("core")
    leaf = 4 * y + jnp.right_shift(z, 1)
    children = [jnp.right_shift(leaf, 3 - k) for k in range(LEVELS)]
    nodes = [(1 << k) - 1 + jnp.right_shift(children[k], 1) for k in range(LEVELS)]
    sides = [jnp.bitwise_and(child, 1) for child in children]
    where = jnp.stack([*nodes, *sides, core, z, y]).astype(jnp.int32)

    left = left_factors.reshape(LEVELS * POINTS, RANK)
    right = right_factors.reshape(LEVELS * POINTS, RANK)
    targets_t = targets.T

    other_features = flipped(train_features, "core", 1)
    sums = gram(targets_t, left, right, test_features)
    sums = block_sum(where, exchange(sums, ("x", "core")))
    send, near, tests = plane_sum(where, exchange(sums, "z"))
    all_tests = [tests] + [flipped(tests, "y", k) for k in (1, 2, 3)]
    far = exchange(send, "y")
    pieces = node_solve(where, far, near, capacitance, pivots.reshape(-1, 1, 2 * RANK))
    solved, weights = update(exchange(pieces, ("x", "core")), targets_t, left)
    other_weights = flipped(weights, "core", 1)
    terms = predict(where, all_tests, train_features, other_features, weights, other_weights)
    predictions = final_sum(exchange(terms, ("y", "z", "x")))
    return solved.T, predictions


def solution(mesh):
    axes = ("y", "z", "x", "core")
    fine = Mesh(mesh.devices.reshape(4, 8, 4, 2), axes)
    rows = P(axes, None)
    factors = P(axes, None, None)
    return jax.shard_map(
        body,
        mesh=fine,
        in_specs=(rows, rows, rows, factors, factors, P(), P()),
        out_specs=(rows, rows),
        check_vma=False,
    )
```

```python
import functools
import math

import jax
import jax.numpy as jnp
from jax import lax
from jax.experimental import pallas as pl
from jax.experimental.pallas import tpu as pltpu
from jax.sharding import Mesh, PartitionSpec as P

LEVELS = 4
RANK = 128
FEAT = 128
TARGETS = 64
POINTS = 1024
SPREAD = 3.0
CUTS = (0, 8, 32, 72, 128)

f32 = jnp.float32
bf16 = jnp.bfloat16
NT = (((1,), (1,)), ((), ()))
NN = (((1,), (0,)), ((), ()))


def params(limit=12):
    return pltpu.CompilerParams(vmem_limit_bytes=limit * 1024 * 1024)


def split2(value):
    high = value.astype(bf16)
    return high, (value - high.astype(f32)).astype(bf16)


def dot3(a, b, dims):
    def one(p, q):
        return lax.dot_general(p, q, dims, preferred_element_type=f32)

    return one(a[0], b[0]) + (one(a[0], b[1]) + one(a[1], b[0]))


def gram_kernel(targets_hbm, left_hbm, right_hbm, out_ref, targets, left, right, upper, lower, sems):
    count = targets.shape[2]
    steps = targets.shape[0]
    loads = []
    for k in range(steps):
        rows = pl.ds(LEVELS * count * k, LEVELS * count)
        pairs = (
            (left_hbm.at[rows], left.at[k]),
            (right_hbm.at[rows], right.at[k]),
            (targets_hbm.at[:, pl.ds(count * k, count)], targets.at[k]),
        )
        loads.append([pltpu.make_async_copy(*p, sems.at[3 * k + n]) for n, p in enumerate(pairs)])
        for load in loads[k]:
            load.start()

    for k in range(steps):
        for load in loads[k]:
            load.wait()

        def level(ref, index):
            return ref[k, pl.ds(index, count, stride=LEVELS), :]

        rows = jnp.concatenate([targets[k]] + [level(left, n).T for n in range(3)], axis=0)
        high, low = split2(rows)
        parts = [split2(level(right, n)) for n in range(LEVELS)]
        pair = lambda i, j: tuple(jnp.concatenate([parts[i][p], parts[j][p]], axis=1) for p in (0, 1))
        first = dot3((high[:192], low[:192]), pair(0, 1), NN)
        second = dot3((high, low), pair(2, 3), NN)
        if k == 0:
            upper[...] = first
            lower[...] = second
        else:
            upper[...] += first
            lower[...] += second

    for n in range(8):
        block = jnp.concatenate(
            [
                upper[8 * n : 8 * n + 8, :RANK],
                upper[24 * n : 24 * n + 24, RANK:],
                lower[40 * n : 40 * n + 40, :RANK],
                lower[56 * n : 56 * n + 56, RANK:],
            ],
            axis=0,
        )
        out_ref[n] = block.astype(bf16)


def gram(targets_t, left, right):
    chunk = 256
    steps = POINTS // chunk
    return pl.pallas_call(
        gram_kernel,
        in_specs=[pl.BlockSpec(memory_space=pltpu.HBM)] * 3,
        out_specs=pl.BlockSpec(memory_space=pltpu.VMEM),
        out_shape=jax.ShapeDtypeStruct((8, 128, RANK), bf16),
        scratch_shapes=[
            pltpu.VMEM((steps, TARGETS, chunk), f32),
            pltpu.VMEM((steps, LEVELS * chunk, RANK), f32),
            pltpu.VMEM((steps, LEVELS * chunk, RANK), f32),
            pltpu.VMEM((192, 256), f32),
            pltpu.VMEM((448, 256), f32),
            pltpu.SemaphoreType.DMA((3 * steps,)),
        ],
        compiler_params=params(60),
        name="gram",
    )(targets_t, left, right)


def block_sum_kernel(in_ref, tests_ref, out_ref):
    total = in_ref[0].astype(f32)
    for n in range(1, 8):
        total += in_ref[n].astype(f32)
    total = total.astype(bf16)
    for n in range(8):
        out_ref[n, :128] = total
        out_ref[n, 128:] = tests_ref[...]


def block_sum(arrived, tests):
    return pl.pallas_call(
        block_sum_kernel,
        out_shape=jax.ShapeDtypeStruct((8, 160, RANK), bf16),
        compiler_params=params(),
        name="block_sum",
    )(arrived, tests)


def plane_sum_kernel(where, in_ref, send_ref, near_ref):
    z = where[8]
    pair = jnp.right_shift(z, 1)

    def rows(index):
        return in_ref[index, :128].astype(f32)

    whole = [rows(k) for k in range(8)]
    below = (whole[0] + whole[1]) + (whole[2] + whole[3])
    above = (whole[4] + whole[5]) + (whole[6] + whole[7])
    send = (below + above)[:32].astype(bf16)
    for k in range(4):
        send_ref[k, :32] = send
        for j in range(8):
            send_ref[k, 32 + 32 * j : 64 + 32 * j] = in_ref[j, 128:]
    odd, even = 2 * jnp.bitwise_or(pair, 1), 2 * jnp.bitwise_and(pair, 2)
    near_ref[0, :40] = above[32:72]
    near_ref[1, :40] = below[32:72]
    near_ref[0, 40:] = (rows(odd) + rows(odd + 1))[72:]
    near_ref[1, 40:] = (rows(even) + rows(even + 1))[72:]


def plane_sum(where, arrived):
    return pl.pallas_call(
        plane_sum_kernel,
        grid_spec=pltpu.PrefetchScalarGridSpec(
            num_scalar_prefetch=1,
            grid=(1,),
            in_specs=[pl.BlockSpec((8, 160, RANK), lambda i, w: (0, 0, 0))],
            out_specs=[
                pl.BlockSpec((4, 288, RANK), lambda i, w: (0, 0, 0)),
                pl.BlockSpec((2, 96, RANK), lambda i, w: (0, 0, 0)),
            ],
        ),
        out_shape=[
            jax.ShapeDtypeStruct((4, 288, RANK), bf16),
            jax.ShapeDtypeStruct((2, 96, RANK), f32),
        ],
        compiler_params=params(),
        name="plane_sum",
    )(where, arrived)


def node_kernel(where, far_ref, near_ref, capacitance, *refs):
    pivots, out_ref, caps, sems = refs
    loads = [
        pltpu.make_async_copy(
            capacitance.at[where[k], pl.ds(pl.multiple_of(RANK * where[4 + k], RANK), RANK)],
            caps.at[k],
            sems.at[k],
        )
        for k in range(LEVELS)
    ]
    for load in loads:
        load.start()
    y = where[9]

    def far(index):
        return far_ref[index, :32].astype(f32)

    stacks = [
        ((far(2) + far(3))[:8], (far(0) + far(1))[:8]),
        (far(jnp.bitwise_or(y, 1))[8:], far(jnp.bitwise_and(y, 2))[8:]),
        (near_ref[0, :40], near_ref[1, :40]),
        (near_ref[0, 40:], near_ref[1, 40:]),
    ]
    solved = []
    for level in range(LEVELS):
        stacked = split2(jnp.concatenate(stacks[level], axis=1))
        source = lax.broadcasted_iota(jnp.int32, (256, 256), 0)
        picks = jnp.where(source == pivots[pl.ds(where[level], 1), :], 1.0, 0.0).astype(bf16)
        moved = [
            lax.dot_general(piece, picks, NN, preferred_element_type=f32).astype(bf16)
            for piece in stacked
        ]
        loads[level].wait()
        solved.append(dot3(moved, split2(caps[level]), NT))
    block = jnp.concatenate(solved, axis=0).astype(bf16)
    for n in range(8):
        out_ref[n] = block


def node_solve(where, far, near, capacitance, pivots):
    return pl.pallas_call(
        node_kernel,
        grid_spec=pltpu.PrefetchScalarGridSpec(
            num_scalar_prefetch=1,
            grid=(1,),
            in_specs=[
                pl.BlockSpec((4, 288, RANK), lambda i, w: (0, 0, 0)),
                pl.BlockSpec((2, 96, RANK), lambda i, w: (0, 0, 0)),
                pl.BlockSpec(memory_space=pltpu.HBM),
                pl.BlockSpec((15, 2 * RANK), lambda i, w: (0, 0)),
            ],
            out_specs=pl.BlockSpec((8, 128, RANK), lambda i, w: (0, 0, 0)),
            scratch_shapes=[
                pltpu.VMEM((LEVELS, RANK, 2 * RANK), f32),
                pltpu.SemaphoreType.DMA((LEVELS,)),
            ],
        ),
        out_shape=jax.ShapeDtypeStruct((8, 128, RANK), bf16),
        compiler_params=params(52),
        name="node_solve",
    )(where, far, near, capacitance, pivots)


def update_kernel(
    pieces_ref, targets_ref, left_ref, mark, out_ref, weights_ref, shares_high, shares_low
):
    del mark
    count = targets_ref.shape[1]

    @pl.when(pl.program_id(0) == 0)
    def _():
        pieces = [pieces_ref[n].astype(f32) for n in range(8)]
        shares = []
        for level in range(LEVELS):
            rows = jnp.concatenate([p[CUTS[level] : CUTS[level + 1]] for p in pieces], axis=0)
            share = rows[:TARGETS]
            for k in range(level):
                begin = TARGETS + RANK * k
                share -= dot3(shares[k], split2(rows[begin : begin + RANK]), NN)
            shares.append(split2(share))
        shares_high[...] = jnp.concatenate([s[0] for s in shares], axis=1)
        shares_low[...] = jnp.concatenate([s[1] for s in shares], axis=1)

    left = [split2(left_ref[pl.ds(k, count, stride=LEVELS), :]) for k in range(LEVELS)]
    joined = [jnp.concatenate([part[p] for part in left], axis=1) for p in (0, 1)]
    value = targets_ref[...] - dot3((shares_high[...], shares_low[...]), joined, NT)
    out_ref[...] = value
    rounded = value.astype(bf16)
    for k in range(4):
        weights_ref[k] = rounded


def update(pieces, targets_t, left, mark):
    chunk = 512
    return pl.pallas_call(
        update_kernel,
        grid=(POINTS // chunk,),
        in_specs=[
            pl.BlockSpec((8, 128, RANK), lambda i: (0, 0, 0)),
            pl.BlockSpec((TARGETS, chunk), lambda i: (0, i)),
            pl.BlockSpec((LEVELS * chunk, RANK), lambda i: (i, 0)),
            pl.BlockSpec(memory_space=pl.ANY),
        ],
        out_specs=[
            pl.BlockSpec((TARGETS, chunk), lambda i: (0, i)),
            pl.BlockSpec((4, TARGETS, chunk), lambda i: (0, 0, i)),
        ],
        out_shape=[
            jax.ShapeDtypeStruct((TARGETS, POINTS), f32),
            jax.ShapeDtypeStruct((4, TARGETS, POINTS), bf16),
        ],
        scratch_shapes=[
            pltpu.VMEM((TARGETS, LEVELS * RANK), bf16),
            pltpu.VMEM((TARGETS, LEVELS * RANK), bf16),
        ],
        compiler_params=params(),
        name="update",
    )(pieces, targets_t, left, mark)


def widened(points, norm_at, one_at):
    value = points.astype(f32)
    norm = -0.5 * jnp.sum(value * value, axis=1, keepdims=True)
    high = norm.astype(bf16).astype(f32)
    middle = (norm - high).astype(bf16).astype(f32)
    low = norm - high - middle
    lane = lax.broadcasted_iota(jnp.int32, points.shape, 1)
    extra = jnp.where((lane >= one_at) & (lane < one_at + 3), 1.0, 0.0)
    for k, piece in enumerate((high, middle, low)):
        extra = jnp.where(lane == norm_at + k, piece, extra)
    return jnp.concatenate([points, extra.astype(bf16)], axis=1)


def block_kernel(tests_ref, *refs):
    features, (out, mark, tests, points, train, slots, sems) = refs[:4], refs[4:]
    mark[...] = jnp.zeros_like(mark)
    loads = [
        pltpu.make_async_copy(features[j], points.at[j], sems.at[j]) for j in range(4)
    ]
    for load in loads:
        load.start()
    for k in range(4):
        tests[256 * k : 256 * k + 256] = widened(tests_ref[k, 32:], 3, 0)
    scale = 2.0 * SPREAD / FEAT * math.log2(math.e)
    stores = []
    for j in range(4):
        loads[j].wait()
        for q in range(4):
            rows = slice(256 * q, 256 * q + 256)
            train[rows] = widened(points[j, rows], 0, 3)
            for i in range(2):
                columns = slice(512 * i, 512 * i + 512)
                inner = lax.dot_general(
                    train[rows], tests[columns], NT, preferred_element_type=f32
                )
                slots[j, rows, columns] = jnp.exp2(inner * scale).astype(bf16)
            part = pl.ds(256 * q, 256)
            stores.append(
                pltpu.make_async_copy(
                    slots.at[j, part], out.at[j, part], sems.at[4 + 4 * j + q]
                )
            )
            stores[-1].start()
    for store in stores:
        store.wait()


def kernel_block(tests, features):
    return pl.pallas_call(
        block_kernel,
        in_specs=[pl.BlockSpec(memory_space=pltpu.VMEM)]
        + [pl.BlockSpec(memory_space=pl.ANY)] * 4,
        out_specs=[pl.BlockSpec(memory_space=pl.ANY), pl.BlockSpec(memory_space=pltpu.VMEM)],
        out_shape=[jax.ShapeDtypeStruct((4, POINTS, 1024), bf16), jax.ShapeDtypeStruct((8, 128), f32)],
        scratch_shapes=[
            pltpu.VMEM((1024, 2 * FEAT), bf16),
            pltpu.VMEM((4, POINTS, FEAT), bf16),
            pltpu.VMEM((POINTS, 2 * FEAT), bf16),
            pltpu.VMEM((4, POINTS, 1024), bf16),
            pltpu.SemaphoreType.DMA((20,)),
        ],
        compiler_params=params(51),
        cost_estimate=pl.CostEstimate(
            flops=2 * 4 * POINTS * 1024 * 256, bytes_accessed=10 << 20, transcendentals=4 << 20
        ),
        name="kernel_block",
    )(tests, *features)


def apply_kernel(where, *refs, last):
    x = where[10]
    if last:
        block, weights_ref, before_ref, out_ref, total, slots, sems = refs
    else:
        block, weights_ref, _, total, slots, sems = refs
    loads = []
    for j in range(4):
        for q in range(4):
            part = pl.ds(256 * q, 256)
            loads.append(
                pltpu.make_async_copy(block.at[j, part], slots.at[j, part], sems.at[4 * j + q])
            )
            loads[-1].start()
    for j in range(4):
        for load in loads[4 * j : 4 * j + 4]:
            load.wait()
        for i in range(4):
            columns = slice(256 * i, 256 * i + 256)
            part = lax.dot_general(
                weights_ref[jnp.bitwise_xor(x, j)], slots[j, :, columns], NN, preferred_element_type=f32
            )
            if j == 0:
                total[:, columns] = part + before_ref[:, columns] if last else part
            else:
                total[:, columns] += part
    if last:
        for i in range(4):
            terms = total[:, 256 * i : 256 * i + 256].T
            for k in range(8):
                rows = [terms[32 * k + 16 * h : 32 * k + 16 * h + 16] for h in (0, 1)]
                out_ref[8 * i + k] = jnp.concatenate(rows, axis=1).astype(bf16)


def apply_block(where, block, weights, before=None, mark=None):
    vmem = pl.BlockSpec(memory_space=pltpu.VMEM)
    last = before is not None
    total = pltpu.VMEM((TARGETS, 1024), f32)
    return pl.pallas_call(
        functools.partial(apply_kernel, last=last),
        in_specs=[pl.BlockSpec(memory_space=pltpu.SMEM), pl.BlockSpec(memory_space=pl.ANY), vmem]
        + [vmem if last else pl.BlockSpec(memory_space=pl.ANY)],
        out_specs=vmem,
        out_shape=jax.ShapeDtypeStruct((32, 16, 128) if last else (TARGETS, 1024), bf16 if last else f32),
        scratch_shapes=[total] * last
        + [pltpu.VMEM((4, POINTS, 1024), bf16), pltpu.SemaphoreType.DMA((16,))],
        compiler_params=params(51),
        cost_estimate=pl.CostEstimate(
            flops=2 * 4 * POINTS * 1024 * 256, bytes_accessed=9 << 20, transcendentals=0
        ),
        name="apply_block",
    )(where, block, weights, before if last else mark)


def final_kernel(in_ref, out_ref):
    total = in_ref[0].astype(f32)
    for k in range(1, 32):
        total += in_ref[k].astype(f32)
    out_ref[:16] = total[:, :TARGETS]
    out_ref[16:] = total[:, TARGETS:]


def final_sum(arrived):
    return pl.pallas_call(
        final_kernel,
        out_shape=jax.ShapeDtypeStruct((32, TARGETS), f32),
        compiler_params=params(),
        name="final_sum",
    )(arrived)


def exchange(blocks, axes):
    return lax.all_to_all(blocks, axes, 0, 0, tiled=True)


def flipped(value, axis, mask):
    return lax.ppermute(value, axis, [(s, s ^ mask) for s in range(lax.axis_size(axis))])


def body(targets, train_features, test_features, left_factors, right_factors, capacitance, pivots):
    y, z = lax.axis_index("y"), lax.axis_index("z")
    leaf = 4 * y + jnp.right_shift(z, 1)
    children = [jnp.right_shift(leaf, 3 - k) for k in range(LEVELS)]
    nodes = [(1 << k) - 1 + jnp.right_shift(children[k], 1) for k in range(LEVELS)]
    sides = [jnp.bitwise_and(child, 1) for child in children]
    where = jnp.stack([*nodes, *sides, z, y, lax.axis_index("x")]).astype(jnp.int32)

    left = left_factors.reshape(LEVELS * POINTS, RANK)
    right = right_factors.reshape(LEVELS * POINTS, RANK)
    targets_t = targets.T

    arrived = exchange(gram(targets_t, left, right), ("x", "core"))
    arrived, own = lax.optimization_barrier((arrived, train_features))
    own = [own] + [flipped(own, "x", k) for k in (1, 2, 3)]
    other = [flipped(part, "core", 1) for part in own]
    planes = exchange(block_sum(arrived, test_features), "z")
    send, near = plane_sum(where, planes)
    far = exchange(send, "y")
    pieces = node_solve(where, far, near, capacitance, pivots)
    pieces = exchange(pieces, ("x", "core"))
    own_block, own_mark = kernel_block(far, own)
    solved, weights = update(pieces, targets_t, left, own_mark)
    weights = exchange(weights, "x")
    other_block, other_mark = kernel_block(far, other)
    weights, other_mark = lax.optimization_barrier((weights, other_mark))
    other_weights = flipped(weights, "core", 1)
    terms = apply_block(where, own_block, weights, mark=other_mark)
    terms = apply_block(where, other_block, other_weights, before=terms)
    predictions = final_sum(exchange(terms, ("y", "z")))
    return solved.T, predictions


def solution(mesh):
    axes = ("y", "z", "x", "core")
    fine = Mesh(mesh.devices.reshape(4, 8, 4, 2), axes)
    rows = P(axes, None)
    factors = P(axes, None, None)
    return jax.shard_map(
        body,
        mesh=fine,
        in_specs=(rows, rows, rows, factors, factors, P(), P()),
        out_specs=(rows, rows),
        check_vma=False,
    )
```

```python
import functools
import math

import jax
import jax.numpy as jnp
from jax import lax
from jax.experimental import pallas as pl
from jax.experimental.pallas import tpu as pltpu
from jax.sharding import Mesh, PartitionSpec as P

LEVELS = 4
RANK = 128
FEAT = 128
TARGETS = 64
POINTS = 1024
SPREAD = 3.0
CUTS = (0, 8, 32, 72, 128)

f32 = jnp.float32
bf16 = jnp.bfloat16
NT = (((1,), (1,)), ((), ()))
NN = (((1,), (0,)), ((), ()))


def params(limit=12):
    return pltpu.CompilerParams(vmem_limit_bytes=limit * 1024 * 1024)


def split2(value):
    high = value.astype(bf16)
    return high, (value - high.astype(f32)).astype(bf16)


def dot3(a, b, dims):
    def one(p, q):
        return lax.dot_general(p, q, dims, preferred_element_type=f32)

    return one(a[0], b[0]) + (one(a[0], b[1]) + one(a[1], b[0]))


def dot2(a, b):
    high = lax.dot_general(a[0], b, NN, preferred_element_type=f32)
    return high + lax.dot_general(a[1], b, NN, preferred_element_type=f32)


def gram_kernel(targets_hbm, left_hbm, right_hbm, out_ref, targets, left, right, upper, lower, sems):
    count = targets.shape[2]
    steps = targets.shape[0]
    loads = []
    for k in range(steps):
        rows = pl.ds(LEVELS * count * k, LEVELS * count)
        pairs = (
            (left_hbm.at[rows], left.at[k]),
            (right_hbm.at[rows], right.at[k]),
            (targets_hbm.at[:, pl.ds(count * k, count)], targets.at[k]),
        )
        loads.append([pltpu.make_async_copy(*p, sems.at[3 * k + n]) for n, p in enumerate(pairs)])
        for load in loads[k]:
            load.start()

    for k in range(steps):
        for load in loads[k]:
            load.wait()

        def level(ref, index):
            return ref[k, pl.ds(index, count, stride=LEVELS), :]

        rows = jnp.concatenate([targets[k]] + [level(left, n).T for n in range(3)], axis=0)
        high, low = split2(rows)
        parts = [level(right, n).astype(bf16) for n in range(LEVELS)]
        first = dot2((high[:192], low[:192]), jnp.concatenate(parts[:2], axis=1))
        second = dot2((high, low), jnp.concatenate(parts[2:], axis=1))
        if k == 0:
            upper[...] = first
            lower[...] = second
        else:
            upper[...] += first
            lower[...] += second

    for n in range(8):
        block = jnp.concatenate(
            [
                upper[8 * n : 8 * n + 8, :RANK],
                upper[24 * n : 24 * n + 24, RANK:],
                lower[40 * n : 40 * n + 40, :RANK],
                lower[56 * n : 56 * n + 56, RANK:],
            ],
            axis=0,
        )
        out_ref[n] = block.astype(bf16)


def gram(targets_t, left, right):
    chunk = 256
    steps = POINTS // chunk
    return pl.pallas_call(
        gram_kernel,
        in_specs=[pl.BlockSpec(memory_space=pltpu.HBM)] * 3,
        out_specs=pl.BlockSpec(memory_space=pltpu.VMEM),
        out_shape=jax.ShapeDtypeStruct((8, 128, RANK), bf16),
        scratch_shapes=[
            pltpu.VMEM((steps, TARGETS, chunk), f32),
            pltpu.VMEM((steps, LEVELS * chunk, RANK), f32),
            pltpu.VMEM((steps, LEVELS * chunk, RANK), f32),
            pltpu.VMEM((192, 256), f32),
            pltpu.VMEM((448, 256), f32),
            pltpu.SemaphoreType.DMA((3 * steps,)),
        ],
        compiler_params=params(60),
        name="gram",
    )(targets_t, left, right)


def block_sum_kernel(in_ref, tests_ref, out_ref):
    total = in_ref[0].astype(f32)
    for n in range(1, 8):
        total += in_ref[n].astype(f32)
    total = total.astype(bf16)
    for n in range(8):
        out_ref[n, :128] = total
        out_ref[n, 128:] = tests_ref[...]


def block_sum(arrived, tests):
    return pl.pallas_call(
        block_sum_kernel,
        out_shape=jax.ShapeDtypeStruct((8, 160, RANK), bf16),
        compiler_params=params(),
        name="block_sum",
    )(arrived, tests)


def plane_sum_kernel(where, in_ref, send_ref, near_ref):
    z = where[8]
    pair = jnp.right_shift(z, 1)

    def rows(index):
        return in_ref[index, :128].astype(f32)

    whole = [rows(k) for k in range(8)]
    below = (whole[0] + whole[1]) + (whole[2] + whole[3])
    above = (whole[4] + whole[5]) + (whole[6] + whole[7])
    send = (below + above)[:32].astype(bf16)
    for k in range(4):
        send_ref[k, :32] = send
        for j in range(8):
            send_ref[k, 32 + 32 * j : 64 + 32 * j] = in_ref[j, 128:]
    odd, even = 2 * jnp.bitwise_or(pair, 1), 2 * jnp.bitwise_and(pair, 2)
    near_ref[0, :40] = above[32:72]
    near_ref[1, :40] = below[32:72]
    near_ref[0, 40:] = (rows(odd) + rows(odd + 1))[72:]
    near_ref[1, 40:] = (rows(even) + rows(even + 1))[72:]


def plane_sum(where, arrived):
    return pl.pallas_call(
        plane_sum_kernel,
        grid_spec=pltpu.PrefetchScalarGridSpec(
            num_scalar_prefetch=1,
            grid=(1,),
            in_specs=[pl.BlockSpec((8, 160, RANK), lambda i, w: (0, 0, 0))],
            out_specs=[
                pl.BlockSpec((4, 288, RANK), lambda i, w: (0, 0, 0)),
                pl.BlockSpec((2, 96, RANK), lambda i, w: (0, 0, 0)),
            ],
        ),
        out_shape=[
            jax.ShapeDtypeStruct((4, 288, RANK), bf16),
            jax.ShapeDtypeStruct((2, 96, RANK), f32),
        ],
        compiler_params=params(),
        name="plane_sum",
    )(where, arrived)


def factor_kernel(where, capacitance, pivots, high, low, caps, sems):
    loads = [
        pltpu.make_async_copy(
            capacitance.at[where[k], pl.ds(pl.multiple_of(RANK * where[4 + k], RANK), RANK)],
            caps.at[k],
            sems.at[k],
        )
        for k in range(LEVELS)
    ]
    for load in loads:
        load.start()
    source = lax.broadcasted_iota(jnp.int32, (256, 256), 0)
    for k in range(LEVELS):
        picks = jnp.where(source == pivots[pl.ds(where[k], 1), :], 1.0, 0.0).astype(bf16)
        loads[k].wait()
        for ref, piece in zip((high, low), split2(caps[k])):
            ref[k] = lax.dot_general(picks, piece, NT, preferred_element_type=f32).astype(bf16)


def node_factors(where, capacitance, pivots):
    vmem = pl.BlockSpec(memory_space=pltpu.VMEM)
    return pl.pallas_call(
        factor_kernel,
        in_specs=[
            pl.BlockSpec(memory_space=pltpu.SMEM),
            pl.BlockSpec(memory_space=pltpu.HBM),
            vmem,
        ],
        out_specs=[vmem] * 2,
        out_shape=[jax.ShapeDtypeStruct((LEVELS, 2 * RANK, RANK), bf16)] * 2,
        scratch_shapes=[
            pltpu.VMEM((LEVELS, RANK, 2 * RANK), f32),
            pltpu.SemaphoreType.DMA((LEVELS,)),
        ],
        compiler_params=params(52),
        name="node_factors",
    )(where, capacitance, pivots)


def node_kernel(where, far_ref, near_ref, high, low, out_ref):
    y = where[9]

    def far(index):
        return far_ref[index, :32].astype(f32)

    stacks = [
        ((far(2) + far(3))[:8], (far(0) + far(1))[:8]),
        (far(jnp.bitwise_or(y, 1))[8:], far(jnp.bitwise_and(y, 2))[8:]),
        (near_ref[0, :40], near_ref[1, :40]),
        (near_ref[0, 40:], near_ref[1, 40:]),
    ]
    solved = [
        dot3(split2(jnp.concatenate(stacks[k], axis=1)), (high[k], low[k]), NN)
        for k in range(LEVELS)
    ]
    block = jnp.concatenate(solved, axis=0).astype(bf16)
    for n in range(8):
        out_ref[n] = block


def node_solve(where, far, near, factors):
    vmem = pl.BlockSpec(memory_space=pltpu.VMEM)
    return pl.pallas_call(
        node_kernel,
        in_specs=[pl.BlockSpec(memory_space=pltpu.SMEM)] + [vmem] * 4,
        out_specs=vmem,
        out_shape=jax.ShapeDtypeStruct((8, 128, RANK), bf16),
        compiler_params=params(),
        name="node_solve",
    )(where, far, near, *factors)


def update_kernel(
    pieces_ref, targets_ref, left_ref, mark, out_ref, weights_ref, shares_high, shares_low
):
    del mark
    count = targets_ref.shape[1]

    @pl.when(pl.program_id(0) == 0)
    def _():
        pieces = [pieces_ref[n].astype(f32) for n in range(8)]
        shares = []
        for level in range(LEVELS):
            rows = jnp.concatenate([p[CUTS[level] : CUTS[level + 1]] for p in pieces], axis=0)
            share = rows[:TARGETS]
            for k in range(level):
                begin = TARGETS + RANK * k
                factor = rows[begin : begin + RANK].astype(bf16)
                for part in shares[k]:
                    share -= lax.dot_general(part, factor, NN, preferred_element_type=f32)
            shares.append(split2(share))
        shares_high[...] = jnp.concatenate([s[0] for s in shares], axis=1)
        shares_low[...] = jnp.concatenate([s[1] for s in shares], axis=1)

    left = [split2(left_ref[pl.ds(k, count, stride=LEVELS), :]) for k in range(LEVELS)]
    joined = [jnp.concatenate([part[p] for part in left], axis=1) for p in (0, 1)]
    value = targets_ref[...] - dot3((shares_high[...], shares_low[...]), joined, NT)
    out_ref[...] = value
    weights_ref[...] = value.astype(bf16)


def update(pieces, targets_t, left, mark):
    chunk = 512
    return pl.pallas_call(
        update_kernel,
        grid=(POINTS // chunk,),
        in_specs=[
            pl.BlockSpec((8, 128, RANK), lambda i: (0, 0, 0)),
            pl.BlockSpec((TARGETS, chunk), lambda i: (0, i)),
            pl.BlockSpec((LEVELS * chunk, RANK), lambda i: (i, 0)),
            pl.BlockSpec(memory_space=pl.ANY),
        ],
        out_specs=[
            pl.BlockSpec((TARGETS, chunk), lambda i: (0, i)),
            pl.BlockSpec((TARGETS, chunk), lambda i: (0, i)),
        ],
        out_shape=[
            jax.ShapeDtypeStruct((TARGETS, POINTS), f32),
            jax.ShapeDtypeStruct((TARGETS, POINTS), bf16),
        ],
        scratch_shapes=[
            pltpu.VMEM((TARGETS, LEVELS * RANK), bf16),
            pltpu.VMEM((TARGETS, LEVELS * RANK), bf16),
        ],
        compiler_params=params(),
        name="update",
    )(pieces, targets_t, left, mark)


def widened(points, norm_at, one_at):
    value = points.astype(f32)
    norm = -0.5 * jnp.sum(value * value, axis=1, keepdims=True)
    high = norm.astype(bf16).astype(f32)
    middle = (norm - high).astype(bf16).astype(f32)
    low = norm - high - middle
    lane = lax.broadcasted_iota(jnp.int32, points.shape, 1)
    extra = jnp.where((lane >= one_at) & (lane < one_at + 3), 1.0, 0.0)
    for k, piece in enumerate((high, middle, low)):
        extra = jnp.where(lane == norm_at + k, piece, extra)
    return jnp.concatenate([points, extra.astype(bf16)], axis=1)


def tests_kernel(in_ref, out_ref):
    for k in range(4):
        out_ref[256 * k : 256 * k + 256] = widened(in_ref[k, 32:], 3, 0)


def widen_tests(far):
    return pl.pallas_call(
        tests_kernel,
        out_shape=jax.ShapeDtypeStruct((1024, 2 * FEAT), bf16),
        compiler_params=params(),
        name="widen_tests",
    )(far)


SCALE = 2.0 * SPREAD / FEAT * math.log2(math.e)


def block_kernel(tests, *refs, whole):
    features, (out, mark, points, train, slots, sems) = refs[:4], refs[4:]
    mark[...] = jnp.zeros_like(mark)
    loads = [
        pltpu.make_async_copy(features[j], points.at[j], sems.at[j]) for j in range(4)
    ]
    for load in loads:
        load.start()
    stores = []
    for j in range(4):
        loads[j].wait()
        for q in range(4):
            rows = slice(256 * q, 256 * q + 256)
            train[j % 2, rows] = widened(points[j, rows], 0, 3)
            for i in range(2):
                columns = slice(512 * i, 512 * i + 512)
                inner = lax.dot_general(
                    train[j % 2, rows], tests[columns], NT, preferred_element_type=f32
                )
                slots[j, rows, columns] = jnp.exp2(inner * SCALE).astype(bf16)
            part = pl.ds(0, POINTS) if whole else pl.ds(256 * q, 256)
            if q == 3 or not whole:
                stores.append(
                    pltpu.make_async_copy(
                        slots.at[j, part], out.at[j, part], sems.at[4 + 4 * j + q]
                    )
                )
                stores[-1].start()
    for store in stores:
        store.wait()


def kernel_block(tests, features, limit, whole):
    vmem = pl.BlockSpec(memory_space=pltpu.VMEM)
    return pl.pallas_call(
        functools.partial(block_kernel, whole=whole),
        in_specs=[vmem] + [pl.BlockSpec(memory_space=pl.ANY)] * 4,
        out_specs=[pl.BlockSpec(memory_space=pl.ANY), vmem],
        out_shape=[
            jax.ShapeDtypeStruct((4, POINTS, 1024), bf16),
            jax.ShapeDtypeStruct((8, 128), f32),
        ],
        scratch_shapes=[
            pltpu.VMEM((4, POINTS, FEAT), bf16),
            pltpu.VMEM((2, POINTS, 2 * FEAT), bf16),
            pltpu.VMEM((4, POINTS, 1024), bf16),
            pltpu.SemaphoreType.DMA((20,)),
        ],
        compiler_params=params(limit),
        cost_estimate=pl.CostEstimate(
            flops=2 * 4 * POINTS * 1024 * 256,
            bytes_accessed=10 << 20,
            transcendentals=4 << 20,
        ),
        name="kernel_block",
    )(tests, *features)


def apply_kernel(block, *refs, last):
    weights, refs = refs[:4], refs[4:]
    if last:
        before_ref, out_ref, total, slots, sems = refs
    else:
        _, total, slots, sems = refs
    loads = []
    for j in range(4):
        for q in range(4):
            part = pl.ds(256 * q, 256)
            loads.append(
                pltpu.make_async_copy(block.at[j, part], slots.at[j, part], sems.at[4 * j + q])
            )
            loads[-1].start()
    for j in range(4):
        for load in loads[4 * j : 4 * j + 4]:
            load.wait()
        for i in range(4):
            columns = slice(256 * i, 256 * i + 256)
            part = lax.dot_general(
                weights[j][...], slots[j, :, columns], NN, preferred_element_type=f32
            )
            if j == 0:
                total[:, columns] = part + before_ref[:, columns] if last else part
            else:
                total[:, columns] += part
    if last:
        for i in range(4):
            terms = total[:, 256 * i : 256 * i + 256].T
            for k in range(8):
                rows = [terms[32 * k + 16 * h : 32 * k + 16 * h + 16] for h in (0, 1)]
                out_ref[8 * i + k] = jnp.concatenate(rows, axis=1).astype(bf16)


def apply_block(block, weights, before=None, mark=None):
    vmem = pl.BlockSpec(memory_space=pltpu.VMEM)
    last = before is not None
    total = pltpu.VMEM((TARGETS, 1024), f32)
    return pl.pallas_call(
        functools.partial(apply_kernel, last=last),
        in_specs=[pl.BlockSpec(memory_space=pl.ANY)]
        + [vmem] * 4
        + [vmem if last else pl.BlockSpec(memory_space=pl.ANY)],
        out_specs=vmem,
        out_shape=jax.ShapeDtypeStruct((32, 16, 128) if last else (TARGETS, 1024), bf16 if last else f32),
        scratch_shapes=[total] * last
        + [pltpu.VMEM((4, POINTS, 1024), bf16), pltpu.SemaphoreType.DMA((16,))],
        compiler_params=params(32 if last else 44),
        cost_estimate=pl.CostEstimate(
            flops=2 * 4 * POINTS * 1024 * 256, bytes_accessed=9 << 20, transcendentals=0
        ),
        name="apply_block",
    )(block, *weights, before if last else mark)


def final_kernel(in_ref, out_ref):
    total = in_ref[0].astype(f32)
    for k in range(1, 32):
        total += in_ref[k].astype(f32)
    out_ref[:16] = total[:, :TARGETS]
    out_ref[16:] = total[:, TARGETS:]


def final_sum(arrived):
    return pl.pallas_call(
        final_kernel,
        out_shape=jax.ShapeDtypeStruct((32, TARGETS), f32),
        compiler_params=params(),
        name="final_sum",
    )(arrived)


def exchange(blocks, axes):
    return lax.all_to_all(blocks, axes, 0, 0, tiled=True)


def flipped(value, axis, mask):
    return lax.ppermute(value, axis, [(s, s ^ mask) for s in range(lax.axis_size(axis))])


def body(targets, train_features, test_features, left_factors, right_factors, capacitance, pivots):
    y, z = lax.axis_index("y"), lax.axis_index("z")
    leaf = 4 * y + jnp.right_shift(z, 1)
    children = [jnp.right_shift(leaf, 3 - k) for k in range(LEVELS)]
    nodes = [(1 << k) - 1 + jnp.right_shift(children[k], 1) for k in range(LEVELS)]
    sides = [jnp.bitwise_and(child, 1) for child in children]
    where = jnp.stack([*nodes, *sides, z, y]).astype(jnp.int32)

    left = left_factors.reshape(LEVELS * POINTS, RANK)
    right = right_factors.reshape(LEVELS * POINTS, RANK)
    targets_t = targets.T

    arrived = exchange(gram(targets_t, left, right), ("x", "core"))
    arrived, own = lax.optimization_barrier((arrived, train_features))
    own = [own] + [flipped(own, "x", k) for k in (1, 2, 3)]
    other = [flipped(part, "core", 1) for part in own]
    planes = exchange(block_sum(arrived, test_features), "z")
    send, near = plane_sum(where, planes)
    far = exchange(send, "y")
    pieces = node_solve(where, far, near, node_factors(where, capacitance, pivots))
    pieces = exchange(pieces, ("x", "core"))
    tests = widen_tests(far)
    own_block, own_mark = kernel_block(tests, own, 51, False)
    solved, weights = update(pieces, targets_t, left, own_mark)
    weights = [weights] + [flipped(weights, "x", k) for k in (1, 2, 3)]
    other_block, other_mark = kernel_block(tests, other, 32, True)
    *weights[1:], other_mark = lax.optimization_barrier((*weights[1:], other_mark))
    other_weights = [flipped(part, "core", 1) for part in weights]
    terms = apply_block(own_block, weights, mark=other_mark)
    terms = apply_block(other_block, other_weights, before=terms)
    predictions = final_sum(exchange(terms, ("y", "z")))
    return solved.T, predictions


def solution(mesh):
    axes = ("y", "z", "x", "core")
    fine = Mesh(mesh.devices.reshape(4, 8, 4, 2), axes)
    rows = P(axes, None)
    factors = P(axes, None, None)
    return jax.shard_map(
        body,
        mesh=fine,
        in_specs=(rows, rows, rows, factors, factors, P(), P()),
        out_specs=(rows, rows),
        check_vma=False,
    )
```

```python
import functools
import math

import jax
import jax.numpy as jnp
from jax import lax
from jax.experimental import pallas as pl
from jax.experimental.pallas import tpu as pltpu
from jax.sharding import Mesh, PartitionSpec as P

LEVELS = 4
RANK = 128
FEAT = 128
TARGETS = 64
POINTS = 1024
SPREAD = 3.0
CUTS = (0, 8, 32, 72, 128)

f32 = jnp.float32
bf16 = jnp.bfloat16
NT = (((1,), (1,)), ((), ()))
NN = (((1,), (0,)), ((), ()))


def params(limit=12):
    return pltpu.CompilerParams(vmem_limit_bytes=limit * 1024 * 1024)


def split2(value):
    high = value.astype(bf16)
    return high, (value - high.astype(f32)).astype(bf16)


def dot3(a, b, dims):
    def one(p, q):
        return lax.dot_general(p, q, dims, preferred_element_type=f32)

    return one(a[0], b[0]) + (one(a[0], b[1]) + one(a[1], b[0]))


def dot2(a, b):
    high = lax.dot_general(a[0], b, NN, preferred_element_type=f32)
    return high + lax.dot_general(a[1], b, NN, preferred_element_type=f32)


def gram_kernel(targets_hbm, left_hbm, right_hbm, out_ref, targets, left, right, upper, lower, sems):
    count = targets.shape[2]
    steps = targets.shape[0]
    loads = []
    for k in range(steps):
        rows = pl.ds(LEVELS * count * k, LEVELS * count)
        pairs = (
            (left_hbm.at[rows], left.at[k]),
            (right_hbm.at[rows], right.at[k]),
            (targets_hbm.at[:, pl.ds(count * k, count)], targets.at[k]),
        )
        loads.append([pltpu.make_async_copy(*p, sems.at[3 * k + n]) for n, p in enumerate(pairs)])
        for load in loads[k]:
            load.start()

    for k in range(steps):
        for load in loads[k]:
            load.wait()

        def level(ref, index):
            return ref[k, pl.ds(index, count, stride=LEVELS), :]

        rows = jnp.concatenate([targets[k]] + [level(left, n).T for n in range(3)], axis=0)
        high, low = split2(rows)
        parts = [level(right, n).astype(bf16) for n in range(LEVELS)]
        first = dot2((high[:192], low[:192]), jnp.concatenate(parts[:2], axis=1))
        second = dot2((high, low), jnp.concatenate(parts[2:], axis=1))
        if k == 0:
            upper[...] = first
            lower[...] = second
        else:
            upper[...] += first
            lower[...] += second

    for n in range(8):
        block = jnp.concatenate(
            [
                upper[8 * n : 8 * n + 8, :RANK],
                upper[24 * n : 24 * n + 24, RANK:],
                lower[40 * n : 40 * n + 40, :RANK],
                lower[56 * n : 56 * n + 56, RANK:],
            ],
            axis=0,
        )
        out_ref[n] = block.astype(bf16)


def gram(targets_t, left, right):
    chunk = 256
    steps = POINTS // chunk
    return pl.pallas_call(
        gram_kernel,
        in_specs=[pl.BlockSpec(memory_space=pltpu.HBM)] * 3,
        out_specs=pl.BlockSpec(memory_space=pltpu.VMEM),
        out_shape=jax.ShapeDtypeStruct((8, 128, RANK), bf16),
        scratch_shapes=[
            pltpu.VMEM((steps, TARGETS, chunk), f32),
            pltpu.VMEM((steps, LEVELS * chunk, RANK), f32),
            pltpu.VMEM((steps, LEVELS * chunk, RANK), f32),
            pltpu.VMEM((192, 256), f32),
            pltpu.VMEM((448, 256), f32),
            pltpu.SemaphoreType.DMA((3 * steps,)),
        ],
        compiler_params=params(60),
        name="gram",
    )(targets_t, left, right)


def block_sum_kernel(in_ref, tests_ref, out_ref):
    total = in_ref[0].astype(f32)
    for n in range(1, 8):
        total += in_ref[n].astype(f32)
    total = total.astype(bf16)
    for n in range(8):
        out_ref[n, :128] = total
        out_ref[n, 128:] = tests_ref[...]


def block_sum(arrived, tests):
    return pl.pallas_call(
        block_sum_kernel,
        out_shape=jax.ShapeDtypeStruct((8, 160, RANK), bf16),
        compiler_params=params(),
        name="block_sum",
    )(arrived, tests)


def plane_sum_kernel(where, in_ref, ready, send_ref, near_ref):
    del ready
    z = where[8]
    pair = jnp.right_shift(z, 1)

    def rows(index):
        return in_ref[index, :128].astype(f32)

    whole = [rows(k) for k in range(8)]
    below = (whole[0] + whole[1]) + (whole[2] + whole[3])
    above = (whole[4] + whole[5]) + (whole[6] + whole[7])
    send = (below + above)[:32].astype(bf16)
    send_ref[:32] = send
    for j in range(8):
        send_ref[32 + 32 * j : 64 + 32 * j] = in_ref[j, 128:]
    odd, even = 2 * jnp.bitwise_or(pair, 1), 2 * jnp.bitwise_and(pair, 2)
    near_ref[0, :40] = above[32:72]
    near_ref[1, :40] = below[32:72]
    near_ref[0, 40:] = (rows(odd) + rows(odd + 1))[72:]
    near_ref[1, 40:] = (rows(even) + rows(even + 1))[72:]


def plane_sum(where, arrived, ready):
    return pl.pallas_call(
        plane_sum_kernel,
        grid_spec=pltpu.PrefetchScalarGridSpec(
            num_scalar_prefetch=1,
            grid=(1,),
            in_specs=[
                pl.BlockSpec((8, 160, RANK), lambda i, w: (0, 0, 0)),
                pl.BlockSpec(memory_space=pl.ANY),
            ],
            out_specs=[
                pl.BlockSpec((288, RANK), lambda i, w: (0, 0)),
                pl.BlockSpec((2, 96, RANK), lambda i, w: (0, 0, 0)),
            ],
        ),
        out_shape=[
            jax.ShapeDtypeStruct((288, RANK), bf16),
            jax.ShapeDtypeStruct((2, 96, RANK), f32),
        ],
        compiler_params=params(),
        name="plane_sum",
    )(where, arrived, ready)


def factor_kernel(where, capacitance, pivots, high, low, caps, sems):
    loads = [
        pltpu.make_async_copy(
            capacitance.at[where[k], pl.ds(pl.multiple_of(RANK * where[4 + k], RANK), RANK)],
            caps.at[k],
            sems.at[k],
        )
        for k in range(LEVELS)
    ]
    for load in loads:
        load.start()
    source = lax.broadcasted_iota(jnp.int32, (256, 256), 0)
    for k in range(LEVELS):
        picks = jnp.where(source == pivots[pl.ds(where[k], 1), :], 1.0, 0.0).astype(bf16)
        loads[k].wait()
        for ref, piece in zip((high, low), split2(caps[k])):
            ref[k] = lax.dot_general(picks, piece, NT, preferred_element_type=f32).astype(bf16)


def node_factors(where, capacitance, pivots):
    vmem = pl.BlockSpec(memory_space=pltpu.VMEM)
    return pl.pallas_call(
        factor_kernel,
        in_specs=[
            pl.BlockSpec(memory_space=pltpu.SMEM),
            pl.BlockSpec(memory_space=pltpu.HBM),
            vmem,
        ],
        out_specs=[vmem] * 2,
        out_shape=[jax.ShapeDtypeStruct((LEVELS, 2 * RANK, RANK), bf16)] * 2,
        scratch_shapes=[
            pltpu.VMEM((LEVELS, RANK, 2 * RANK), f32),
            pltpu.SemaphoreType.DMA((LEVELS,)),
        ],
        compiler_params=params(52),
        name="node_factors",
    )(where, capacitance, pivots)


def node_kernel(where, near_ref, high, low, *refs):
    far, out_ref = [ref[:32].astype(f32) for ref in refs[:4]], refs[4]
    y = where[9]

    def ordered(own, other, odd):
        return jnp.where(odd == 1, own, other), jnp.where(odd == 1, other, own)

    stacks = [
        ordered((far[0] + far[1])[:8], (far[2] + far[3])[:8], jnp.right_shift(y, 1)),
        ordered(far[0][8:], far[1][8:], jnp.bitwise_and(y, 1)),
        (near_ref[0, :40], near_ref[1, :40]),
        (near_ref[0, 40:], near_ref[1, 40:]),
    ]
    solved = [
        dot3(split2(jnp.concatenate(stacks[k], axis=1)), (high[k], low[k]), NN)
        for k in range(LEVELS)
    ]
    block = jnp.concatenate(solved, axis=0).astype(bf16)
    for n in range(8):
        out_ref[n] = block


def node_solve(where, far, near, factors):
    vmem = pl.BlockSpec(memory_space=pltpu.VMEM)
    return pl.pallas_call(
        node_kernel,
        in_specs=[pl.BlockSpec(memory_space=pltpu.SMEM)] + [vmem] * 7,
        out_specs=vmem,
        out_shape=jax.ShapeDtypeStruct((8, 128, RANK), bf16),
        compiler_params=params(),
        name="node_solve",
    )(where, near, *factors, *far)


def update_kernel(
    pieces_ref, targets_ref, left_ref, mark, out_ref, weights_ref, shares_high, shares_low
):
    del mark
    count = targets_ref.shape[1]

    @pl.when(pl.program_id(0) == 0)
    def _():
        pieces = [pieces_ref[n].astype(f32) for n in range(8)]
        shares = []
        for level in range(LEVELS):
            rows = jnp.concatenate([p[CUTS[level] : CUTS[level + 1]] for p in pieces], axis=0)
            share = rows[:TARGETS]
            for k in range(level):
                begin = TARGETS + RANK * k
                factor = rows[begin : begin + RANK].astype(bf16)
                for part in shares[k]:
                    share -= lax.dot_general(part, factor, NN, preferred_element_type=f32)
            shares.append(split2(share))
        shares_high[...] = jnp.concatenate([s[0] for s in shares], axis=1)
        shares_low[...] = jnp.concatenate([s[1] for s in shares], axis=1)

    left = [split2(left_ref[pl.ds(k, count, stride=LEVELS), :]) for k in range(LEVELS)]
    joined = [jnp.concatenate([part[p] for part in left], axis=1) for p in (0, 1)]
    value = targets_ref[...] - dot3((shares_high[...], shares_low[...]), joined, NT)
    out_ref[...] = value
    weights_ref[...] = value.astype(bf16)


def update(pieces, targets_t, left, mark):
    chunk = 512
    return pl.pallas_call(
        update_kernel,
        grid=(POINTS // chunk,),
        in_specs=[
            pl.BlockSpec((8, 128, RANK), lambda i: (0, 0, 0)),
            pl.BlockSpec((TARGETS, chunk), lambda i: (0, i)),
            pl.BlockSpec((LEVELS * chunk, RANK), lambda i: (i, 0)),
            pl.BlockSpec(memory_space=pl.ANY),
        ],
        out_specs=[
            pl.BlockSpec((TARGETS, chunk), lambda i: (0, i)),
            pl.BlockSpec((TARGETS, chunk), lambda i: (0, i)),
        ],
        out_shape=[
            jax.ShapeDtypeStruct((TARGETS, POINTS), f32),
            jax.ShapeDtypeStruct((TARGETS, POINTS), bf16),
        ],
        scratch_shapes=[
            pltpu.VMEM((TARGETS, LEVELS * RANK), bf16),
            pltpu.VMEM((TARGETS, LEVELS * RANK), bf16),
        ],
        compiler_params=params(),
        name="update",
    )(pieces, targets_t, left, mark)


def widened(points, norm_at, one_at):
    value = points.astype(f32)
    norm = -0.5 * jnp.sum(value * value, axis=1, keepdims=True)
    high = norm.astype(bf16).astype(f32)
    middle = (norm - high).astype(bf16).astype(f32)
    low = norm - high - middle
    lane = lax.broadcasted_iota(jnp.int32, points.shape, 1)
    extra = jnp.where((lane >= one_at) & (lane < one_at + 3), 1.0, 0.0)
    for k, piece in enumerate((high, middle, low)):
        extra = jnp.where(lane == norm_at + k, piece, extra)
    return jnp.concatenate([points, extra.astype(bf16)], axis=1)


def tests_kernel(where, *refs):
    for k in range(4):
        at = pl.multiple_of(256 * jnp.bitwise_xor(where[9], k), 256)
        refs[4][pl.ds(at, 256)] = widened(refs[k][32:], 3, 0)


def widen_tests(where, far):
    return pl.pallas_call(
        tests_kernel,
        in_specs=[pl.BlockSpec(memory_space=pltpu.SMEM)]
        + [pl.BlockSpec(memory_space=pltpu.VMEM)] * 4,
        out_specs=pl.BlockSpec(memory_space=pltpu.VMEM),
        out_shape=jax.ShapeDtypeStruct((1024, 2 * FEAT), bf16),
        compiler_params=params(),
        name="widen_tests",
    )(where, *far)


SCALE = 2.0 * SPREAD / FEAT * math.log2(math.e)


def block_kernel(tests, *refs, whole):
    features, (out, mark, points, train, slots, sems) = refs[:4], refs[4:]
    mark[...] = jnp.zeros_like(mark)
    loads = [
        pltpu.make_async_copy(features[j], points.at[j], sems.at[j]) for j in range(4)
    ]
    for load in loads:
        load.start()
    stores = []
    for j in range(4):
        loads[j].wait()
        for q in range(4):
            rows = slice(256 * q, 256 * q + 256)
            train[j % 2, rows] = widened(points[j, rows], 0, 3)
            for i in range(2):
                columns = slice(512 * i, 512 * i + 512)
                inner = lax.dot_general(
                    train[j % 2, rows], tests[columns], NT, preferred_element_type=f32
                )
                slots[j, rows, columns] = jnp.exp2(inner * SCALE).astype(bf16)
            part = pl.ds(0, POINTS) if whole else pl.ds(256 * q, 256)
            if q == 3 or not whole:
                stores.append(
                    pltpu.make_async_copy(
                        slots.at[j, part], out.at[j, part], sems.at[4 + 4 * j + q]
                    )
                )
                stores[-1].start()
    for store in stores:
        store.wait()


def kernel_block(tests, features, limit, whole):
    vmem = pl.BlockSpec(memory_space=pltpu.VMEM)
    return pl.pallas_call(
        functools.partial(block_kernel, whole=whole),
        in_specs=[vmem] + [pl.BlockSpec(memory_space=pl.ANY)] * 4,
        out_specs=[pl.BlockSpec(memory_space=pl.ANY), vmem],
        out_shape=[
            jax.ShapeDtypeStruct((4, POINTS, 1024), bf16),
            jax.ShapeDtypeStruct((8, 128), f32),
        ],
        scratch_shapes=[
            pltpu.VMEM((4, POINTS, FEAT), bf16),
            pltpu.VMEM((2, POINTS, 2 * FEAT), bf16),
            pltpu.VMEM((4, POINTS, 1024), bf16),
            pltpu.SemaphoreType.DMA((20,)),
        ],
        compiler_params=params(limit),
        cost_estimate=pl.CostEstimate(
            flops=2 * 4 * POINTS * 1024 * 256,
            bytes_accessed=10 << 20,
            transcendentals=4 << 20,
        ),
        name="kernel_block",
    )(tests, *features)


def apply_kernel(block, *refs, last):
    weights, refs = refs[:4], refs[4:]
    if last:
        before_ref, out_ref, total, slots, sems = refs
    else:
        _, total, slots, sems = refs
    loads = []
    for j in range(4):
        for q in range(4):
            part = pl.ds(256 * q, 256)
            loads.append(
                pltpu.make_async_copy(block.at[j, part], slots.at[j, part], sems.at[4 * j + q])
            )
            loads[-1].start()
    for j in range(4):
        for load in loads[4 * j : 4 * j + 4]:
            load.wait()
        for i in range(4):
            columns = slice(256 * i, 256 * i + 256)
            part = lax.dot_general(
                weights[j][...], slots[j, :, columns], NN, preferred_element_type=f32
            )
            if j == 0:
                total[:, columns] = part + before_ref[:, columns] if last else part
            else:
                total[:, columns] += part
    if last:
        for i in range(4):
            terms = total[:, 256 * i : 256 * i + 256].T
            for k in range(8):
                rows = [terms[32 * k + 16 * h : 32 * k + 16 * h + 16] for h in (0, 1)]
                out_ref[8 * i + k] = jnp.concatenate(rows, axis=1).astype(bf16)


def apply_block(block, weights, before=None, mark=None):
    vmem = pl.BlockSpec(memory_space=pltpu.VMEM)
    last = before is not None
    total = pltpu.VMEM((TARGETS, 1024), f32)
    return pl.pallas_call(
        functools.partial(apply_kernel, last=last),
        in_specs=[pl.BlockSpec(memory_space=pl.ANY)]
        + [vmem] * 4
        + [vmem if last else pl.BlockSpec(memory_space=pl.ANY)],
        out_specs=vmem,
        out_shape=jax.ShapeDtypeStruct((32, 16, 128) if last else (TARGETS, 1024), bf16 if last else f32),
        scratch_shapes=[total] * last
        + [pltpu.VMEM((4, POINTS, 1024), bf16), pltpu.SemaphoreType.DMA((16,))],
        compiler_params=params(32 if last else 44),
        cost_estimate=pl.CostEstimate(
            flops=2 * 4 * POINTS * 1024 * 256, bytes_accessed=9 << 20, transcendentals=0
        ),
        name="apply_block",
    )(block, *weights, before if last else mark)


def final_kernel(in_ref, out_ref):
    total = in_ref[0].astype(f32)
    for k in range(1, 32):
        total += in_ref[k].astype(f32)
    out_ref[:16] = total[:, :TARGETS]
    out_ref[16:] = total[:, TARGETS:]


def final_sum(arrived):
    return pl.pallas_call(
        final_kernel,
        out_shape=jax.ShapeDtypeStruct((32, TARGETS), f32),
        compiler_params=params(),
        name="final_sum",
    )(arrived)


def exchange(blocks, axes):
    return lax.all_to_all(blocks, axes, 0, 0, tiled=True)


def flipped(value, axis, mask):
    return lax.ppermute(value, axis, [(s, s ^ mask) for s in range(lax.axis_size(axis))])


def body(targets, train_features, test_features, left_factors, right_factors, capacitance, pivots):
    y, z = lax.axis_index("y"), lax.axis_index("z")
    leaf = 4 * y + jnp.right_shift(z, 1)
    children = [jnp.right_shift(leaf, 3 - k) for k in range(LEVELS)]
    nodes = [(1 << k) - 1 + jnp.right_shift(children[k], 1) for k in range(LEVELS)]
    sides = [jnp.bitwise_and(child, 1) for child in children]
    where = jnp.stack([*nodes, *sides, z, y]).astype(jnp.int32)

    left = left_factors.reshape(LEVELS * POINTS, RANK)
    right = right_factors.reshape(LEVELS * POINTS, RANK)
    targets_t = targets.T

    arrived = exchange(gram(targets_t, left, right), ("x", "core"))
    arrived, own = lax.optimization_barrier((arrived, train_features))
    own = [own] + [flipped(own, "x", k) for k in (1, 2, 3)]
    other = [flipped(part, "core", 1) for part in own]
    planes = exchange(block_sum(arrived, test_features), "z")
    factors = node_factors(where, capacitance, pivots)
    send, near = plane_sum(where, planes, factors[0])
    far = [send] + [flipped(send, "y", k) for k in (1, 2, 3)]
    pieces = node_solve(where, far, near, factors)
    pieces = exchange(pieces, ("x", "core"))
    tests = widen_tests(where, far)
    own_block, own_mark = kernel_block(tests, own, 51, False)
    solved, weights = update(pieces, targets_t, left, own_mark)
    weights = [weights] + [flipped(weights, "x", k) for k in (1, 2, 3)]
    other_block, other_mark = kernel_block(tests, other, 32, True)
    *weights[1:], other_mark = lax.optimization_barrier((*weights[1:], other_mark))
    other_weights = [flipped(part, "core", 1) for part in weights]
    terms = apply_block(own_block, weights, mark=other_mark)
    terms = apply_block(other_block, other_weights, before=terms)
    predictions = final_sum(exchange(terms, ("y", "z")))
    return solved.T, predictions


def solution(mesh):
    axes = ("y", "z", "x", "core")
    fine = Mesh(mesh.devices.reshape(4, 8, 4, 2), axes)
    rows = P(axes, None)
    factors = P(axes, None, None)
    return jax.shard_map(
        body,
        mesh=fine,
        in_specs=(rows, rows, rows, factors, factors, P(), P()),
        out_specs=(rows, rows),
        check_vma=False,
    )
```
